32 devices in a mesh: dp: 8 (over y, x, core), ctx: 4 (over z).
Axes of the slice: x: 2, y: 2, z: 4, core: 2. Of those that a mesh axis runs over, the one named last changes fastest.
Arguments:
- tokens: bfloat16 [2, 8, 1024, 576], P(None, 'dp', 'ctx'), may hold values from -6 to 6
- span_order: int32 [2, 8, 4], P(None, 'dp'), may hold values from 0 to 3, each once within a row
- cotangent: bfloat16 [2, 8, 1024, 576], P(None, 'dp', 'ctx'), may hold values from -6 to 6
- query_weight: bfloat16 [576, 576], P('dp', 'ctx'), may hold values from -0.25 to 0.25
- key_weight: bfloat16 [576, 192], P('dp', 'ctx'), may hold values from -0.25 to 0.25
- value_weight: bfloat16 [576, 192], P('dp', 'ctx'), may hold values from -0.25 to 0.25
- output_weight: bfloat16 [576, 576], P('dp', 'ctx'), may hold values from -1.5 to 1.5
- gate_weight: bfloat16 [576, 1536], P('dp', 'ctx'), may hold values from -0.25 to 0.25
- up_weight: bfloat16 [576, 1536], P('dp', 'ctx'), may hold values from -0.25 to 0.25
- down_weight: bfloat16 [1536, 576], P('dp', 'ctx'), may hold values from -0.15625 to 0.15625
- attention_gain: bfloat16 [576], P('dp'), may hold values from 0.25 to 1.75
- feedforward_gain: bfloat16 [576], P('dp'), may hold values from 0.25 to 1.75
Outputs:
- layer_output: bfloat16 [2, 8, 1024, 576], P(None, 'dp', 'ctx')
- input_grad: float32 [2, 8, 1024, 576], P(None, 'dp', 'ctx')
- query_grad: float32 [576, 576], P('dp', 'ctx')
- key_grad: float32 [576, 192], P('dp', 'ctx')
- value_grad: float32 [576, 192], P('dp', 'ctx')
- output_grad: float32 [576, 576], P('dp', 'ctx')
- gate_grad: float32 [576, 1536], P('dp', 'ctx')
- up_grad: float32 [576, 1536], P('dp', 'ctx')
- down_grad: float32 [1536, 576], P('dp', 'ctx')
- attention_gain_grad: float32 [576], P('dp')
- feedforward_gain_grad: float32 [576], P('dp')
The draws below stay inside these ranges and needn't reach their ends.
Inputs may be any that keep to these rules, and one draw needn't show every extreme that they name: `span_order`: for every micro-batch and sequence the 4 entries are the span numbers 0 to 3, each once.
All inputs are finite; a program needn't handle non-finite values.
Results may differ from the reference program's by a relative error of at most 0.02.
Values may be sent and summed in bfloat16 or wider, within the bound.
A program may use at most 128 MiB of HBM per device.

```python
import jax
import jax.numpy as jnp
from jax import lax

D = 576
HEADS = 9
KV_HEADS = 3
HEAD_DIM = 64
FF = 1536
QD = 576
KVD = 192
SEQ_LEN = 1024
MICRO = 2
SEQS = 8
SPANS = 4
N_CTX = 4


def block_levels(own_key, shape, shards, least, largest):
    gain, own = 1.0, jax.random.fold_in(own_key, 6)
    for dim, parts in shards:
        heights = jnp.exp(jax.random.uniform(jax.random.fold_in(own, dim), (parts,), jnp.float32, least / len(shards), largest / len(shards)))
        gain = gain * jnp.repeat(heights, shape[dim] // parts).reshape([-1 if axis == dim else 1 for axis in range(len(shape))])
    return gain


def scatter_about(own_key, shape, deviation, reach, shards=(), held_as=jnp.bfloat16):
    level = block_levels(own_key, shape, shards, -0.22, 0.18) if shards else 1.0
    entries = jax.random.normal(own_key, shape, jnp.float32) * deviation * level
    return jnp.minimum(jnp.maximum(entries, -reach), reach).astype(held_as)


def setup_inputs(seed: int = 0) -> dict:
    arg_keys = jax.random.split(jax.random.key(seed), 13)
    return {
        "tokens": scatter_about(arg_keys[0], (MICRO, SEQS, SEQ_LEN, D), 1.0, 6.0, ((1, 8), (2, 4))),
        "span_order": jax.vmap(lambda own: jax.random.permutation(own, SPANS))(jax.random.split(arg_keys[1], MICRO * SEQS)).reshape((MICRO, SEQS, SPANS)).astype(jnp.int32),
        "cotangent": scatter_about(arg_keys[2], (MICRO, SEQS, SEQ_LEN, D), 1.0, 6.0, ((1, 8), (2, 4))),
        "query_weight": scatter_about(arg_keys[3], (D, QD), D ** -0.5, 0.25, ((0, 8), (1, 4))),
        "key_weight": scatter_about(arg_keys[4], (D, KVD), D ** -0.5, 0.25, ((0, 8), (1, 4))),
        "value_weight": scatter_about(arg_keys[5], (D, KVD), D ** -0.5, 0.25, ((0, 8), (1, 4))),
        "output_weight": scatter_about(arg_keys[6], (QD, D), (QD // 32) ** -0.5, 1.5, ((0, 8), (1, 4))),
        "gate_weight": scatter_about(arg_keys[7], (D, FF), D ** -0.5, 0.25, ((0, 8), (1, 4))),
        "up_weight": scatter_about(arg_keys[8], (D, FF), D ** -0.5, 0.25, ((0, 8), (1, 4))),
        "down_weight": scatter_about(arg_keys[9], (FF, D), FF ** -0.5, 0.15625, ((0, 8), (1, 4))),
        "attention_gain": jnp.clip(1.0 + 0.15 * jax.random.normal(arg_keys[10], (D,), jnp.float32), 0.25, 1.75).astype(jnp.bfloat16),
        "feedforward_gain": jnp.clip(1.0 + 0.15 * jax.random.normal(arg_keys[11], (D,), jnp.float32), 0.25, 1.75).astype(jnp.bfloat16),
    }


@jax.custom_vjp
def low(v):
    return lax.optimization_barrier(v.astype(jnp.bfloat16)).astype(jnp.float32)

@jax.custom_vjp
def low_back(v):
    return v

def low_keep(v):
    return (low(v), None)

def low_pass(kept, grad):
    return (grad,)

def back_keep(v):
    return (v, None)

def back_low(kept, grad):
    return (low(grad),)
low.defvjp(low_keep, low_pass)
low_back.defvjp(back_keep, back_low)
EPSILON = 1e-05
NEG_FILL = -1e+30
HIGHEST = lax.Precision.HIGHEST

def rotate(values, cos_table, sin_table):
    half_dim = values.shape[-1] // 2
    lower_half = values[..., :half_dim]
    upper_half = values[..., half_dim:]
    return jnp.concatenate([lower_half * cos_table - upper_half * sin_table, upper_half * cos_table + lower_half * sin_table], axis=-1)

def normalize(values, gain_vec):
    inverse_rms = lax.rsqrt(lax.optimization_barrier(jnp.mean(values * values, axis=-1, keepdims=True)) + EPSILON)
    return values * inverse_rms * gain_vec

def decoder_layer(weight_set, sequence, order_row):
    query_mat, key_mat, value_mat, output_mat, gate_mat, up_mat, down_mat, attn_gain, ffn_gain = weight_set
    seq_length = sequence.shape[0]
    span_len = seq_length // N_CTX
    position = (order_row[:, None] * span_len + jnp.arange(span_len, dtype=jnp.int32)[None, :]).reshape(seq_length)
    inverse_freq = 1.0 / 10000.0 ** (jnp.arange(0, HEAD_DIM, 2).astype(jnp.float32) / HEAD_DIM)
    angle_table = position.astype(jnp.float32)[:, None] * inverse_freq[None, :]
    cos_table = jnp.cos(angle_table)[:, None, :]
    sin_table = jnp.sin(angle_table)[:, None, :]
    normed = low(normalize(sequence, attn_gain))
    query_pre = low_back(jnp.dot(normed, query_mat, precision=HIGHEST))
    key_pre = low_back(jnp.dot(normed, key_mat, precision=HIGHEST))
    value_low = low(low_back(jnp.dot(normed, value_mat, precision=HIGHEST)))
    query_rot = low(rotate(query_pre.reshape(seq_length, HEADS, HEAD_DIM), cos_table, sin_table))
    key_rot = low(rotate(key_pre.reshape(seq_length, KV_HEADS, HEAD_DIM), cos_table, sin_table))
    value_heads = value_low.reshape(seq_length, KV_HEADS, HEAD_DIM)
    group_size = HEADS // KV_HEADS
    query_groups = query_rot.reshape(seq_length, KV_HEADS, group_size, HEAD_DIM)
    raw_scores = low_back(jnp.einsum('qhgd,khd->hgqk', query_groups, key_rot, precision=HIGHEST))
    allowed = position[None, :] <= position[:, None]
    scaled = jnp.where(allowed, raw_scores * HEAD_DIM ** (-0.5), NEG_FILL)
    row_peak = lax.optimization_barrier(jnp.max(scaled, axis=-1, keepdims=True))
    exponent = jnp.exp(scaled - row_peak)
    attn_probs = low(exponent / lax.optimization_barrier(jnp.sum(exponent, axis=-1, keepdims=True)))
    mixed = jnp.einsum('hgqk,khd->qhgd', attn_probs, value_heads, precision=HIGHEST).reshape(seq_length, HEADS * HEAD_DIM)
    mixed = low(low_back(mixed))
    middle = sequence + low_back(jnp.dot(mixed, output_mat, precision=HIGHEST))
    hidden = low(normalize(middle, ffn_gain))
    gate_act = low_back(jnp.dot(hidden, gate_mat, precision=HIGHEST))
    up_act = low_back(jnp.dot(hidden, up_mat, precision=HIGHEST))
    inner = low(gate_act * jax.nn.sigmoid(gate_act) * up_act)
    return middle + low_back(jnp.dot(inner, down_mat, precision=HIGHEST))

def reference(tokens, span_order, cotangent, query_weight, key_weight, value_weight, output_weight, gate_weight, up_weight, down_weight, attention_gain, feedforward_gain):
    weight_set = tuple((weight_item.astype(jnp.float32) for weight_item in (query_weight, key_weight, value_weight, output_weight, gate_weight, up_weight, down_weight, attention_gain, feedforward_gain)))
    flat_tokens = tokens.astype(jnp.float32).reshape(MICRO * SEQS, SEQ_LEN, D)
    flat_orders = span_order.reshape(MICRO * SEQS, SPANS)
    flat_cotangent = cotangent.astype(jnp.float32).reshape(MICRO * SEQS, SEQ_LEN, D)

    def forward(weights_in, tokens_in):

        def per_sequence(inputs_pair):
            return decoder_layer(weights_in, inputs_pair[0], inputs_pair[1])
        return lax.map(jax.checkpoint(per_sequence), (tokens_in, flat_orders))
    result, pullback = jax.vjp(forward, weight_set, flat_tokens)
    weight_grads, token_grads = pullback(flat_cotangent)
    full_shape = (MICRO, SEQS, SEQ_LEN, D)
    return (result.reshape(full_shape).astype(jnp.bfloat16), token_grads.reshape(full_shape), weight_grads[0], weight_grads[1], weight_grads[2], weight_grads[3], weight_grads[4], weight_grads[5], weight_grads[6], weight_grads[7], weight_grads[8])
```

```python
import functools

import jax
import jax.numpy as jnp
from jax import lax
from jax.experimental import pallas as pl
from jax.experimental.pallas import tpu as pltpu
from jax.sharding import PartitionSpec as P

HEADS = 9
KV_HEADS = 3
HEAD_DIM = 64


EPSILON = 1e-05
NEG_FILL = -1e30


def rotate(values, cos_table, sin_table):
    half_dim = values.shape[-1] // 2
    lower_half = values[..., :half_dim]
    upper_half = values[..., half_dim:]
    return jnp.concatenate(
        [
            lower_half * cos_table - upper_half * sin_table,
            upper_half * cos_table + lower_half * sin_table,
        ],
        axis=-1,
    )


def unrotate(values, cos_table, sin_table):
    half_dim = values.shape[-1] // 2
    lower_half = values[..., :half_dim]
    upper_half = values[..., half_dim:]
    return jnp.concatenate(
        [
            lower_half * cos_table + upper_half * sin_table,
            upper_half * cos_table - lower_half * sin_table,
        ],
        axis=-1,
    )


def angle_tables(position):
    inverse_freq = 1.0 / 10000.0 ** (jnp.arange(0, HEAD_DIM, 2).astype(jnp.float32) / HEAD_DIM)
    angle_table = position.astype(jnp.float32)[..., None] * inverse_freq
    return (jnp.cos(angle_table)[:, :, None, :], jnp.sin(angle_table)[:, :, None, :])


def rows_product(left_mat, right_mat):
    return lax.dot_general(
        left_mat, right_mat, (((0,), (0,)), ((), ())), preferred_element_type=jnp.float32
    )


def transposed_product(left_mat, right_mat):
    return lax.dot_general(
        left_mat, right_mat, (((1,), (1,)), ((), ())), preferred_element_type=jnp.float32
    )


MESH = pl.DeviceIdType.MESH
VMEM_LIMIT = 56 * 1024 * 1024


def place_on_slice():
    part = lax.axis_index("dp")
    return lax.axis_index("ctx"), part % 2, part // 4, (part // 2) % 2


def device_at(ctx, core, row, col):
    return (row * 4 + col * 2 + core, ctx)


def greet(partners):
    barrier = pltpu.get_barrier_semaphore()
    for partner in partners:
        pl.semaphore_signal(barrier, inc=1, device_id=partner, device_id_type=MESH)
    pl.semaphore_wait(barrier, len(partners))


def remote(source, target, send_sem, recv_sem, device):
    return pltpu.make_async_remote_copy(
        src_ref=source,
        dst_ref=target,
        send_sem=send_sem,
        recv_sem=recv_sem,
        device_id=device,
        device_id_type=MESH,
    )


def gather_kernel(n_ctx, own_ref, all_ref, send_sem, recv_sem):
    ctx, core, row, col = place_on_slice()
    sibling = device_at(ctx, 1 - core, row, col)
    beside = device_at(ctx, core, row, 1 - col)
    across = device_at(ctx, core, 1 - row, col)
    spans = [device_at((ctx + step) % n_ctx, core, row, col) for step in range(1, n_ctx)]
    greet([sibling, beside, across] + spans)
    sent = []

    def send(source, target, group, index, device):
        copy = remote(source, target, send_sem.at[group, index], recv_sem.at[group, index], device)
        copy.start()
        sent.append(copy)

    def arrive(target, group, index):
        remote(
            target, target, send_sem.at[group, index], recv_sem.at[group, index], sibling
        ).wait_recv()

    for step in range(1, n_ctx):
        send(own_ref, all_ref.at[ctx, core, row, col], 0, step, spans[step - 1])
    all_ref[ctx, core, row, col] = own_ref[...]

    def piece(step):
        return (ctx + n_ctx - step) % n_ctx

    def first(step):
        at = piece(step)
        if step:
            arrive(all_ref.at[at, core, row, col], 0, step)
        half_a, half_b = all_ref.at[at, core, row, col, 0], all_ref.at[at, core, row, col, 1]
        send(half_a, half_a, 1, step, beside)
        send(half_b, half_b, 2, step, across)

    def second(step):
        at = piece(step)
        arrive(all_ref.at[at, core, row, 1 - col, 0], 1, step)
        arrive(all_ref.at[at, core, 1 - row, col, 1], 2, step)
        half_a, half_b = all_ref.at[at, core, row, :, 0], all_ref.at[at, core, :, col, 1]
        send(half_a, half_a, 3, step, across)
        send(half_b, half_b, 4, step, beside)

    def third(step):
        at = piece(step)
        arrive(all_ref.at[at, core, 1 - row, :, 0], 3, step)
        arrive(all_ref.at[at, core, :, 1 - col, 1], 4, step)
        send(all_ref.at[at, core], all_ref.at[at, core], 5, step, sibling)

    for tick in range(n_ctx + 2):
        if 0 <= tick - 1 < n_ctx:
            second(tick - 1)
        if 0 <= tick - 2 < n_ctx:
            third(tick - 2)
        if tick < n_ctx:
            first(tick)
    for step in range(n_ctx):
        arrive(all_ref.at[piece(step), 1 - core], 5, step)
    for copy in sent:
        copy.wait_send()


def scatter_kernel(
    n_ctx, term_ref, sum_ref, got_1, part_1, got_2, part_2, got_3, part_3, got_4, send_sem, recv_sem
):
    ctx, core, row, col = place_on_slice()
    sibling = device_at(ctx, 1 - core, row, col)
    beside = device_at(ctx, core, row, 1 - col)
    across = device_at(ctx, core, 1 - row, col)
    spans = [device_at((ctx + step) % n_ctx, core, row, col) for step in range(1, n_ctx)]
    greet([sibling, beside, across] + spans)
    order = list(range(1, n_ctx)) + [0]
    sent = []

    def send(source, target, group, index, device):
        copy = remote(source, target, send_sem.at[group, index], recv_sem.at[group, index], device)
        copy.start()
        sent.append(copy)

    def arrive(target, group, index):
        remote(
            target, target, send_sem.at[group, index], recv_sem.at[group, index], sibling
        ).wait_recv()

    def piece(step):
        return (ctx + step) % n_ctx

    def add(one, two):
        return (one.astype(jnp.float32) + two.astype(jnp.float32)).astype(jnp.bfloat16)

    for step in order:
        send(term_ref.at[piece(step), 1 - core], got_1.at[step], 0, step, sibling)

    def first(step):
        at = piece(step)
        arrive(got_1.at[step], 0, step)

        def body(index, carry):
            r, c, h = index // 4, (index // 2) % 2, index % 2
            part_1[step, r, c, h] = add(term_ref[at, core, r, c, h], got_1[step, r, c, h])
            return carry

        lax.fori_loop(0, 8, body, 0)
        send(part_1.at[step, :, 1 - col, 0], got_2.at[step, 0], 1, step, beside)
        send(part_1.at[step, 1 - row, :, 1], got_2.at[step, 1], 2, step, across)

    def second(step):
        arrive(got_2.at[step, 0], 1, step)
        arrive(got_2.at[step, 1], 2, step)
        for index in range(2):
            part_2[step, 0, index] = add(part_1[step, index, col, 0], got_2[step, 0, index])
            part_2[step, 1, index] = add(part_1[step, row, index, 1], got_2[step, 1, index])
        send(part_2.at[step, 0, 1 - row], got_3.at[step, 0], 3, step, across)
        send(part_2.at[step, 1, 1 - col], got_3.at[step, 1], 4, step, beside)

    def third(step):
        arrive(got_3.at[step, 0], 3, step)
        arrive(got_3.at[step, 1], 4, step)
        part_3[step, 0] = add(part_2[step, 0, row], got_3[step, 0])
        part_3[step, 1] = add(part_2[step, 1, col], got_3[step, 1])
        if step:
            send(part_3.at[step], got_4.at[step], 5, step, spans[step - 1])

    for tick in range(n_ctx + 2):
        if tick < n_ctx:
            first(order[tick])
        if 0 <= tick - 1 < n_ctx:
            second(order[tick - 1])
        if 0 <= tick - 2 < n_ctx:
            third(order[tick - 2])
    for step in range(1, n_ctx):
        arrive(got_4.at[step], 5, step)
    for half in range(2):
        total = part_3[0, half].astype(jnp.float32)
        for step in range(1, n_ctx):
            total = total + got_4[step, half].astype(jnp.float32)
        sum_ref[half] = total
    for copy in sent:
        copy.wait_send()


def span_gather_kernel(n_ctx, own_ref, all_ref, send_sem, recv_sem):
    ctx, core, row, col = place_on_slice()
    spans = [device_at((ctx + step) % n_ctx, core, row, col) for step in range(1, n_ctx)]
    greet(spans)
    copies = []
    for step in range(1, n_ctx):
        copy = remote(
            own_ref, all_ref.at[ctx], send_sem.at[step], recv_sem.at[step], spans[step - 1]
        )
        copy.start()
        copies.append(copy)
    all_ref[ctx] = own_ref[...]
    for step in range(1, n_ctx):
        target = all_ref.at[(ctx + n_ctx - step) % n_ctx]
        remote(target, target, send_sem.at[step], recv_sem.at[step], spans[0]).wait_recv()
    for copy in copies:
        copy.wait_send()


def span_scatter_kernel(n_ctx, term_ref, sum_ref, got_ref, send_sem, recv_sem):
    ctx, core, row, col = place_on_slice()
    spans = [device_at((ctx + step) % n_ctx, core, row, col) for step in range(1, n_ctx)]
    greet(spans)
    copies = []
    for step in range(1, n_ctx):
        copy = remote(
            term_ref.at[(ctx + step) % n_ctx],
            got_ref.at[step],
            send_sem.at[step],
            recv_sem.at[step],
            spans[step - 1],
        )
        copy.start()
        copies.append(copy)
    for step in range(1, n_ctx):
        copies[step - 1].wait_recv()
    total = term_ref[ctx].astype(jnp.float32)
    for step in range(1, n_ctx):
        total = total + got_ref[step].astype(jnp.float32)
    sum_ref[...] = total
    for copy in copies:
        copy.wait_send()


def vmem_call(kernel, operand, out_shape, scratch, collective_id):
    whole = pl.BlockSpec(memory_space=pltpu.VMEM)
    return pl.pallas_call(
        kernel,
        out_shape=out_shape,
        in_specs=[whole],
        out_specs=whole,
        scratch_shapes=scratch,
        compiler_params=pltpu.CompilerParams(
            collective_id=collective_id, has_side_effects=True, vmem_limit_bytes=VMEM_LIMIT
        ),
    )(operand)


def own_plan():
    return lax.axis_size("dp") == 8 and lax.axis_size("ctx") == 4


def span_gather(own):
    n_ctx = lax.axis_size("ctx")
    if not own_plan():
        return lax.all_gather(own, "ctx", axis=0)
    seqs, span, features = own.shape
    sems = pltpu.SemaphoreType.DMA((n_ctx,))
    gathered = vmem_call(
        functools.partial(span_gather_kernel, n_ctx),
        own.reshape(seqs * span, features),
        jax.ShapeDtypeStruct((n_ctx, seqs * span, features), own.dtype),
        [sems, sems],
        1,
    )
    return gathered.reshape(n_ctx, seqs, span, features)


def span_scatter(terms):
    n_ctx, seqs, span, features = terms.shape
    if not own_plan():
        return lax.psum_scatter(terms, "ctx", scatter_dimension=0).astype(jnp.float32)
    sems = pltpu.SemaphoreType.DMA((n_ctx,))
    summed = vmem_call(
        functools.partial(span_scatter_kernel, n_ctx),
        terms.reshape(n_ctx, seqs * span, features),
        jax.ShapeDtypeStruct((seqs * span, features), jnp.float32),
        [pltpu.VMEM((n_ctx, seqs * span, features), terms.dtype), sems, sems],
        2,
    )
    return summed.reshape(seqs, span, features)


def all_shards(packed):
    n_dp, n_ctx = lax.axis_size("dp"), lax.axis_size("ctx")
    if not own_plan():
        return lax.all_gather(packed, ("dp", "ctx"), axis=0).reshape(n_dp, n_ctx, *packed.shape)
    sems = pltpu.SemaphoreType.DMA((6, n_ctx))
    gathered = vmem_call(
        functools.partial(gather_kernel, n_ctx),
        packed,
        jax.ShapeDtypeStruct((n_ctx, 2, 2, 2) + packed.shape, packed.dtype),
        [sems, sems],
        3,
    )
    return gathered.transpose(2, 3, 1, 0, 4, 5, 6).reshape(n_dp, n_ctx, *packed.shape)


def sum_shards(terms):
    n_dp, n_ctx = terms.shape[:2]
    shard = terms.shape[2:]
    if not own_plan():
        part = lax.psum_scatter(terms, "dp", scatter_dimension=0)
        return lax.psum_scatter(part, "ctx", scatter_dimension=0).astype(jnp.float32)
    sems = pltpu.SemaphoreType.DMA((6, n_ctx))
    return vmem_call(
        functools.partial(scatter_kernel, n_ctx),
        terms.reshape(2, 2, 2, n_ctx, *shard).transpose(3, 2, 0, 1, 4, 5, 6),
        jax.ShapeDtypeStruct(shard, jnp.float32),
        [
            pltpu.VMEM((n_ctx, 2, 2) + shard, terms.dtype),
            pltpu.VMEM((n_ctx, 2, 2) + shard, terms.dtype),
            pltpu.VMEM((n_ctx, 2, 2) + shard[1:], terms.dtype),
            pltpu.VMEM((n_ctx, 2, 2) + shard[1:], terms.dtype),
            pltpu.VMEM((n_ctx,) + shard, terms.dtype),
            pltpu.VMEM((n_ctx,) + shard, terms.dtype),
            pltpu.VMEM((n_ctx,) + shard, terms.dtype),
            sems,
            sems,
        ],
        4,
    )


GAIN_ROWS = 8


def gather_weights(
    query_weight,
    key_weight,
    value_weight,
    output_weight,
    gate_weight,
    up_weight,
    down_weight,
    attention_gain,
    feedforward_gain,
):
    n_dp, n_ctx = lax.axis_size("dp"), lax.axis_size("ctx")
    rows = query_weight.shape[0]
    width = 2 * gate_weight.shape[1]
    blocks = down_weight.shape[1] // rows
    down_side = down_weight.T.reshape(blocks, rows, -1).swapaxes(0, 1).reshape(rows, -1)
    half_a = jnp.concatenate(
        [query_weight, key_weight, value_weight, output_weight, gate_weight], axis=1
    )
    half_b = jnp.concatenate([up_weight, down_side], axis=1)
    gains = jnp.stack([attention_gain, feedforward_gain], axis=0)
    gains = jnp.pad(gains, ((0, GAIN_ROWS - 2), (0, width - rows)))
    packed = jnp.stack(
        [jnp.concatenate([half_a, gains], axis=0), jnp.concatenate([half_b, gains], axis=0)]
    )
    shards = all_shards(packed)

    def whole(half, start, stop):
        part = shards[:, :, half, :rows, start:stop]
        return part.transpose(0, 2, 1, 3).reshape(n_dp * rows, n_ctx * (stop - start))

    mats, start = [], 0
    for item in (query_weight, key_weight, value_weight, output_weight, gate_weight):
        mats.append(whole(0, start, start + item.shape[1]))
        start += item.shape[1]
    mats.append(whole(1, 0, up_weight.shape[1]))
    down_part = shards[:, :, 1, :rows, up_weight.shape[1] :]
    down_part = down_part.reshape(n_dp, n_ctx, rows, blocks, -1).transpose(1, 3, 2, 0, 4)
    mats.append(down_part.reshape(n_ctx * blocks * rows, -1))
    gain_part = shards[:, 0, 0, rows : rows + 2, :rows]
    mats.append(gain_part[:, 0].reshape(-1))
    mats.append(gain_part[:, 1].reshape(-1))
    return tuple(mats)


def scatter_grads(query, key, value, output, gate, up, down_side, attn_gain, ffn_gain):
    n_dp, n_ctx = lax.axis_size("dp"), lax.axis_size("ctx")
    rows = query.shape[0] // n_dp
    width = 2 * gate.shape[1] // n_ctx
    blocks = down_side.shape[0] // (n_ctx * rows)

    def parts(item):
        item = item.astype(jnp.bfloat16)
        return item.reshape(n_dp, rows, n_ctx, -1).transpose(0, 2, 1, 3)

    down_part = down_side.astype(jnp.bfloat16).reshape(n_ctx, blocks, rows, n_dp, -1)
    down_part = down_part.transpose(3, 0, 2, 1, 4).reshape(n_dp, n_ctx, rows, -1)
    half_a = jnp.concatenate([parts(item) for item in (query, key, value, output, gate)], axis=-1)
    half_b = jnp.concatenate([parts(up), down_part], axis=-1)
    gains = jnp.stack([attn_gain.reshape(n_dp, rows), ffn_gain.reshape(n_dp, rows)], axis=1)
    gains = jnp.pad(gains.astype(jnp.bfloat16), ((0, 0), (0, GAIN_ROWS - 2), (0, width - rows)))
    gains = jnp.broadcast_to(gains[:, None], (n_dp, n_ctx, GAIN_ROWS, width))
    terms = jnp.stack(
        [jnp.concatenate([half_a, gains], axis=2), jnp.concatenate([half_b, gains], axis=2)], axis=2
    )
    total = sum_shards(terms)
    grads, start = [], 0
    for item in (query, key, value, output, gate):
        stop = start + item.shape[1] // n_ctx
        grads.append(total[0, :rows, start:stop])
        start = stop
    up_stop = up.shape[1] // n_ctx
    grads.append(total[1, :rows, :up_stop])
    down_own = total[1, :rows, up_stop:].reshape(rows, blocks, -1).swapaxes(0, 1)
    grads.append(down_own.reshape(blocks * rows, -1).T)
    grads.append(total[0, rows, :rows])
    grads.append(total[0, rows + 1, :rows])
    return tuple(grads)


def masked_scores(query_rot, key_all, query_pos, key_pos):
    seq_count, span_len = (query_rot.shape[0], query_rot.shape[1])
    group_size = HEADS // KV_HEADS
    query_groups = query_rot.reshape(seq_count, span_len, KV_HEADS, group_size, HEAD_DIM)
    key_heads = key_all.reshape(seq_count, key_all.shape[1], KV_HEADS, HEAD_DIM)
    raw_scores = jnp.einsum(
        "sqhgd,skhd->shgqk", query_groups, key_heads, preferred_element_type=jnp.float32
    )
    allowed = (key_pos[:, None, :] <= query_pos[:, :, None])[:, None, None, :, :]
    return jnp.where(allowed, raw_scores * HEAD_DIM ** (-0.5), NEG_FILL)


def forward_pass(micro_tokens, micro_order, whole_set, ctx_index):
    query_mat, key_mat, value_mat, output_mat, gate_mat, up_mat, down_mat = whole_set[:7]
    attn_gain = whole_set[7].astype(jnp.float32)
    ffn_gain = whole_set[8].astype(jnp.float32)
    seq_count, span_len, model_width = micro_tokens.shape
    row_count = seq_count * span_len
    ctx_parts = micro_order.shape[1]
    sequence = micro_tokens.astype(jnp.float32).reshape(row_count, model_width)
    inverse_one = lax.rsqrt(jnp.mean(sequence * sequence, axis=-1, keepdims=True) + EPSILON)
    norm_one = sequence * inverse_one
    normed = (norm_one * attn_gain).astype(jnp.bfloat16)
    query_pre = jnp.dot(normed, query_mat, preferred_element_type=jnp.float32)
    key_pre = jnp.dot(normed, key_mat, preferred_element_type=jnp.float32)
    value_low = (
        jnp.dot(normed, value_mat, preferred_element_type=jnp.float32)
        .astype(jnp.bfloat16)
        .reshape(seq_count, span_len, KV_HEADS * HEAD_DIM)
    )
    own_span = lax.dynamic_index_in_dim(micro_order, ctx_index, axis=1, keepdims=False)
    offsets = jnp.arange(span_len, dtype=jnp.int32)
    query_pos = own_span[:, None] * span_len + offsets[None, :]
    key_pos = (micro_order[:, :, None] * span_len + offsets[None, None, :]).reshape(
        seq_count, ctx_parts * span_len
    )
    cos_table, sin_table = angle_tables(query_pos)
    query_rot = rotate(
        query_pre.reshape(seq_count, span_len, HEADS, HEAD_DIM), cos_table, sin_table
    ).astype(jnp.bfloat16)
    key_rot = (
        rotate(key_pre.reshape(seq_count, span_len, KV_HEADS, HEAD_DIM), cos_table, sin_table)
        .astype(jnp.bfloat16)
        .reshape(seq_count, span_len, KV_HEADS * HEAD_DIM)
    )
    kv_width = KV_HEADS * HEAD_DIM
    both_all = span_gather(jnp.concatenate([key_rot, value_low], axis=-1))
    both_all = jnp.swapaxes(both_all, 0, 1).reshape(seq_count, ctx_parts * span_len, 2 * kv_width)
    key_all, value_all = both_all[..., :kv_width], both_all[..., kv_width:]
    scaled = masked_scores(query_rot, key_all, query_pos, key_pos)
    row_peak = jnp.max(scaled, axis=-1, keepdims=True)
    exponent = jnp.exp(scaled - row_peak)
    row_total = jnp.sum(exponent, axis=-1, keepdims=True)
    attn_probs = (exponent / row_total).astype(jnp.bfloat16)
    log_total = row_peak + jnp.log(row_total)
    value_heads = value_all.reshape(seq_count, value_all.shape[1], KV_HEADS, HEAD_DIM)
    mixed = (
        jnp.einsum("shgqk,skhd->sqhgd", attn_probs, value_heads, preferred_element_type=jnp.float32)
        .reshape(row_count, HEADS * HEAD_DIM)
        .astype(jnp.bfloat16)
    )
    middle = sequence + jnp.dot(mixed, output_mat, preferred_element_type=jnp.float32)
    inverse_two = lax.rsqrt(jnp.mean(middle * middle, axis=-1, keepdims=True) + EPSILON)
    norm_two = middle * inverse_two
    hidden = (norm_two * ffn_gain).astype(jnp.bfloat16)
    gate_act = jnp.dot(hidden, gate_mat, preferred_element_type=jnp.float32)
    up_act = jnp.dot(hidden, up_mat, preferred_element_type=jnp.float32)
    sigmoid_gate = jax.nn.sigmoid(gate_act)
    inner = (gate_act * sigmoid_gate * up_act).astype(jnp.bfloat16)
    result = middle + transposed_product(inner, down_mat)
    kept_state = (
        inverse_one,
        norm_one,
        normed,
        query_rot,
        key_all,
        value_all,
        query_pos,
        key_pos,
        cos_table,
        sin_table,
        log_total,
        mixed,
        inverse_two,
        norm_two,
        hidden,
        gate_act,
        up_act,
        sigmoid_gate,
        inner,
    )
    return (result.astype(jnp.bfloat16).reshape(seq_count, span_len, model_width), kept_state)


def backward_pass(micro_cot, kept_state, whole_set):
    query_mat, key_mat, value_mat, output_mat, gate_mat, up_mat, down_mat = whole_set[:7]
    attn_gain = whole_set[7].astype(jnp.float32)
    ffn_gain = whole_set[8].astype(jnp.float32)
    (
        inverse_one,
        norm_one,
        normed,
        query_rot,
        key_all,
        value_all,
        query_pos,
        key_pos,
        cos_table,
        sin_table,
        log_total,
        mixed,
        inverse_two,
        norm_two,
        hidden,
        gate_act,
        up_act,
        sigmoid_gate,
        inner,
    ) = kept_state
    seq_count, span_len, model_width = micro_cot.shape
    row_count = seq_count * span_len
    key_length = key_all.shape[1]
    group_size = HEADS // KV_HEADS
    cot_rows = micro_cot.reshape(row_count, model_width)
    d_inner = jnp.dot(cot_rows, down_mat, preferred_element_type=jnp.float32)
    silu_slope = sigmoid_gate + gate_act * sigmoid_gate * (1.0 - sigmoid_gate)
    d_gate = (d_inner * up_act * silu_slope).astype(jnp.bfloat16)
    d_up = (d_inner * (gate_act * sigmoid_gate)).astype(jnp.bfloat16)
    d_hidden = transposed_product(d_gate, gate_mat) + transposed_product(d_up, up_mat)
    ffn_gain_grad = jnp.sum(d_hidden * norm_two, axis=0)
    d_norm_two = d_hidden * ffn_gain
    d_middle = cot_rows.astype(jnp.float32) + inverse_two * (
        d_norm_two - norm_two * jnp.mean(d_norm_two * norm_two, axis=-1, keepdims=True)
    )
    d_branch = d_middle.astype(jnp.bfloat16)
    d_mixed = (
        transposed_product(d_branch, output_mat)
        .astype(jnp.bfloat16)
        .reshape(seq_count, span_len, KV_HEADS, group_size, HEAD_DIM)
    )
    scaled = masked_scores(query_rot, key_all, query_pos, key_pos)
    attn_probs = jnp.exp(scaled - log_total)
    probs_low = attn_probs.astype(jnp.bfloat16)
    value_heads = value_all.reshape(seq_count, key_length, KV_HEADS, HEAD_DIM)
    key_heads = key_all.reshape(seq_count, key_length, KV_HEADS, HEAD_DIM)
    query_groups = query_rot.reshape(seq_count, span_len, KV_HEADS, group_size, HEAD_DIM)
    d_probs = jnp.einsum(
        "sqhgd,skhd->shgqk", d_mixed, value_heads, preferred_element_type=jnp.float32
    )
    value_term = jnp.einsum(
        "shgqk,sqhgd->skhd", probs_low, d_mixed, preferred_element_type=jnp.float32
    )
    row_delta = jnp.sum(attn_probs * d_probs, axis=-1, keepdims=True)
    d_scores = (HEAD_DIM ** (-0.5) * (attn_probs * (d_probs - row_delta))).astype(jnp.bfloat16)
    d_query_rot = jnp.einsum(
        "shgqk,skhd->sqhgd", d_scores, key_heads, preferred_element_type=jnp.float32
    )
    key_term = jnp.einsum(
        "shgqk,sqhgd->skhd", d_scores, query_groups, preferred_element_type=jnp.float32
    )
    kv_width = KV_HEADS * HEAD_DIM
    both_terms = jnp.concatenate(
        [
            key_term.reshape(seq_count, key_length, kv_width),
            value_term.reshape(seq_count, key_length, kv_width),
        ],
        axis=-1,
    ).astype(jnp.bfloat16)
    both_terms = jnp.swapaxes(
        both_terms.reshape(seq_count, key_length // span_len, -1, 2 * kv_width), 0, 1
    )
    both_sum = span_scatter(both_terms)
    d_key_rot, d_value = both_sum[..., :kv_width], both_sum[..., kv_width:]
    d_query = (
        unrotate(d_query_rot.reshape(seq_count, span_len, HEADS, HEAD_DIM), cos_table, sin_table)
        .reshape(row_count, HEADS * HEAD_DIM)
        .astype(jnp.bfloat16)
    )
    d_key = (
        unrotate(d_key_rot.reshape(seq_count, span_len, KV_HEADS, HEAD_DIM), cos_table, sin_table)
        .reshape(row_count, KV_HEADS * HEAD_DIM)
        .astype(jnp.bfloat16)
    )
    d_value_low = d_value.reshape(row_count, KV_HEADS * HEAD_DIM).astype(jnp.bfloat16)
    d_normed = (
        transposed_product(d_query, query_mat)
        + transposed_product(d_key, key_mat)
        + transposed_product(d_value_low, value_mat)
    )
    attn_gain_grad = jnp.sum(d_normed * norm_one, axis=0)
    d_norm_one = d_normed * attn_gain
    d_tokens = d_middle + inverse_one * (
        d_norm_one - norm_one * jnp.mean(d_norm_one * norm_one, axis=-1, keepdims=True)
    )
    product_rows = (
        normed,
        jnp.concatenate([d_query, d_key, d_value_low], axis=1),
        mixed,
        d_branch,
        hidden,
        jnp.concatenate([d_gate, d_up], axis=1),
        inner,
        cot_rows,
    )
    return (
        d_tokens.reshape(seq_count, span_len, model_width),
        product_rows,
        attn_gain_grad,
        ffn_gain_grad,
    )


def per_device(
    tokens,
    span_order,
    cotangent,
    query_weight,
    key_weight,
    value_weight,
    output_weight,
    gate_weight,
    up_weight,
    down_weight,
    attention_gain,
    feedforward_gain,
):
    ctx_index = lax.axis_index("ctx")
    whole_set = gather_weights(
        query_weight,
        key_weight,
        value_weight,
        output_weight,
        gate_weight,
        up_weight,
        down_weight,
        attention_gain,
        feedforward_gain,
    )
    rows_shape = (-1,) + tokens.shape[2:]
    layer_out, kept_state = forward_pass(
        tokens.reshape(rows_shape),
        span_order.reshape(-1, span_order.shape[-1]),
        whole_set,
        ctx_index,
    )
    token_grad, product_rows, attn_gain_grad, ffn_gain_grad = backward_pass(
        cotangent.reshape(rows_shape), kept_state, whole_set
    )
    normed, d_heads, mixed, d_branch, hidden, d_wide, inner, cot_rows = product_rows
    query_width, kv_width = whole_set[0].shape[1], whole_set[1].shape[1]
    ff_width = whole_set[4].shape[1]
    grads = scatter_grads(
        rows_product(normed, d_heads[:, :query_width]),
        rows_product(normed, d_heads[:, query_width : query_width + kv_width]),
        rows_product(normed, d_heads[:, query_width + kv_width :]),
        rows_product(mixed, d_branch),
        rows_product(hidden, d_wide[:, :ff_width]),
        rows_product(hidden, d_wide[:, ff_width:]),
        rows_product(cot_rows, inner),
        attn_gain_grad,
        ffn_gain_grad,
    )
    return (layer_out.reshape(tokens.shape), token_grad.reshape(tokens.shape)) + grads


def solution(mesh):
    in_specs = (
        P(None, "dp", "ctx", None),
        P(None, "dp", None),
        P(None, "dp", "ctx", None),
        P("dp", "ctx"),
        P("dp", "ctx"),
        P("dp", "ctx"),
        P("dp", "ctx"),
        P("dp", "ctx"),
        P("dp", "ctx"),
        P("dp", "ctx"),
        P("dp"),
        P("dp"),
    )
    out_specs = (
        P(None, "dp", "ctx", None),
        P(None, "dp", "ctx", None),
        P("dp", "ctx"),
        P("dp", "ctx"),
        P("dp", "ctx"),
        P("dp", "ctx"),
        P("dp", "ctx"),
        P("dp", "ctx"),
        P("dp", "ctx"),
        P("dp"),
        P("dp"),
    )
    return jax.shard_map(
        per_device, mesh=mesh, in_specs=in_specs, out_specs=out_specs, check_vma=False
    )
```

```python
import functools

import jax
import jax.numpy as jnp
from jax import lax
from jax.experimental import pallas as pl
from jax.experimental.pallas import tpu as pltpu
from jax.sharding import PartitionSpec as P

HEADS = 9
KV_HEADS = 3
HEAD_DIM = 64


EPSILON = 1e-05
NEG_FILL = -1e30


def rotate(values, cos_table, sin_table):
    half_dim = values.shape[-1] // 2
    lower_half = values[..., :half_dim]
    upper_half = values[..., half_dim:]
    return jnp.concatenate(
        [
            lower_half * cos_table - upper_half * sin_table,
            upper_half * cos_table + lower_half * sin_table,
        ],
        axis=-1,
    )


def unrotate(values, cos_table, sin_table):
    half_dim = values.shape[-1] // 2
    lower_half = values[..., :half_dim]
    upper_half = values[..., half_dim:]
    return jnp.concatenate(
        [
            lower_half * cos_table + upper_half * sin_table,
            upper_half * cos_table - lower_half * sin_table,
        ],
        axis=-1,
    )


def angle_tables(position):
    inverse_freq = 1.0 / 10000.0 ** (jnp.arange(0, HEAD_DIM, 2).astype(jnp.float32) / HEAD_DIM)
    angle_table = position.astype(jnp.float32)[..., None] * inverse_freq
    return (jnp.cos(angle_table)[:, :, None, :], jnp.sin(angle_table)[:, :, None, :])


def rows_product(left_mat, right_mat):
    return lax.dot_general(
        left_mat, right_mat, (((0,), (0,)), ((), ())), preferred_element_type=jnp.float32
    )


def transposed_product(left_mat, right_mat):
    return lax.dot_general(
        left_mat, right_mat, (((1,), (1,)), ((), ())), preferred_element_type=jnp.float32
    )


MESH = pl.DeviceIdType.MESH
VMEM_LIMIT = 56 * 1024 * 1024


def place_on_slice():
    part = lax.axis_index("dp")
    return lax.axis_index("ctx"), part % 2, part // 4, (part // 2) % 2


def device_at(ctx, core, row, col):
    return (row * 4 + col * 2 + core, ctx)


def greet(partners):
    barrier = pltpu.get_barrier_semaphore()
    for partner in partners:
        pl.semaphore_signal(barrier, inc=1, device_id=partner, device_id_type=MESH)
    pl.semaphore_wait(barrier, len(partners))


def remote(source, target, send_sem, recv_sem, device):
    return pltpu.make_async_remote_copy(
        src_ref=source,
        dst_ref=target,
        send_sem=send_sem,
        recv_sem=recv_sem,
        device_id=device,
        device_id_type=MESH,
    )


def gather_kernel(n_ctx, with_spans, *refs):
    if with_spans:
        own_ref, span_ref, all_ref, spans_ref, send_sem, recv_sem, span_send, span_recv = refs
    else:
        own_ref, all_ref, send_sem, recv_sem = refs
    ctx, core, row, col = place_on_slice()
    sibling = device_at(ctx, 1 - core, row, col)
    beside = device_at(ctx, core, row, 1 - col)
    across = device_at(ctx, core, 1 - row, col)
    spans = [device_at((ctx + step) % n_ctx, core, row, col) for step in range(1, n_ctx)]
    greet([sibling, beside, across] + spans)
    sent = []

    def send(source, target, group, index, device):
        copy = remote(source, target, send_sem.at[group, index], recv_sem.at[group, index], device)
        copy.start()
        sent.append(copy)

    def arrive(target, group, index):
        remote(
            target, target, send_sem.at[group, index], recv_sem.at[group, index], sibling
        ).wait_recv()

    for step in range(1, n_ctx):
        send(own_ref, all_ref.at[ctx, core, row, col], 0, step, spans[step - 1])
    all_ref[ctx, core, row, col] = own_ref[...]
    if with_spans:
        for step in range(1, n_ctx):
            copy = remote(
                span_ref,
                spans_ref.at[ctx],
                span_send.at[step],
                span_recv.at[step],
                spans[step - 1],
            )
            copy.start()
            sent.append(copy)
        spans_ref[ctx] = span_ref[...]

    def piece(step):
        return (ctx + n_ctx - step) % n_ctx

    def first(step):
        at = piece(step)
        if step:
            arrive(all_ref.at[at, core, row, col], 0, step)
        half_a, half_b = all_ref.at[at, core, row, col, 0], all_ref.at[at, core, row, col, 1]
        send(half_a, half_a, 1, step, beside)
        send(half_b, half_b, 2, step, across)

    def second(step):
        at = piece(step)
        arrive(all_ref.at[at, core, row, 1 - col, 0], 1, step)
        arrive(all_ref.at[at, core, 1 - row, col, 1], 2, step)
        half_a, half_b = all_ref.at[at, core, row, :, 0], all_ref.at[at, core, :, col, 1]
        send(half_a, half_a, 3, step, across)
        send(half_b, half_b, 4, step, beside)

    def third(step):
        at = piece(step)
        arrive(all_ref.at[at, core, 1 - row, :, 0], 3, step)
        arrive(all_ref.at[at, core, :, 1 - col, 1], 4, step)
        send(all_ref.at[at, core], all_ref.at[at, core], 5, step, sibling)

    for tick in range(n_ctx + 2):
        if 0 <= tick - 1 < n_ctx:
            second(tick - 1)
        if 0 <= tick - 2 < n_ctx:
            third(tick - 2)
        if tick < n_ctx:
            first(tick)
    for step in range(n_ctx):
        arrive(all_ref.at[piece(step), 1 - core], 5, step)
    if with_spans:
        for step in range(1, n_ctx):
            target = spans_ref.at[piece(step)]
            remote(target, target, span_send.at[step], span_recv.at[step], spans[0]).wait_recv()
    for copy in sent:
        copy.wait_send()


def scatter_kernel(n_ctx, with_spans, *refs):
    if with_spans:
        term_ref, span_ref, sum_ref, span_sum, *refs, span_got, span_send, span_recv = refs
    else:
        term_ref, sum_ref, *refs = refs
    got_1, part_1, got_2, part_2, got_3, part_3, got_4, send_sem, recv_sem = refs
    ctx, core, row, col = place_on_slice()
    sibling = device_at(ctx, 1 - core, row, col)
    beside = device_at(ctx, core, row, 1 - col)
    across = device_at(ctx, core, 1 - row, col)
    spans = [device_at((ctx + step) % n_ctx, core, row, col) for step in range(1, n_ctx)]
    greet([sibling, beside, across] + spans)
    order = list(range(1, n_ctx)) + [0]
    sent = []

    def send(source, target, group, index, device):
        copy = remote(source, target, send_sem.at[group, index], recv_sem.at[group, index], device)
        copy.start()
        sent.append(copy)

    def arrive(target, group, index):
        remote(
            target, target, send_sem.at[group, index], recv_sem.at[group, index], sibling
        ).wait_recv()

    def piece(step):
        return (ctx + step) % n_ctx

    def add(one, two):
        return (one.astype(jnp.float32) + two.astype(jnp.float32)).astype(jnp.bfloat16)

    span_copies = []
    if with_spans:
        for step in range(1, n_ctx):
            copy = remote(
                span_ref.at[piece(step)],
                span_got.at[step],
                span_send.at[step],
                span_recv.at[step],
                spans[step - 1],
            )
            copy.start()
            sent.append(copy)
            span_copies.append(copy)
    for step in order:
        send(term_ref.at[piece(step), 1 - core], got_1.at[step], 0, step, sibling)

    def first(step):
        at = piece(step)
        arrive(got_1.at[step], 0, step)

        def body(index, carry):
            r, c, h = index // 4, (index // 2) % 2, index % 2
            part_1[step, r, c, h] = add(term_ref[at, core, r, c, h], got_1[step, r, c, h])
            return carry

        lax.fori_loop(0, 8, body, 0)
        send(part_1.at[step, :, 1 - col, 0], got_2.at[step, 0], 1, step, beside)
        send(part_1.at[step, 1 - row, :, 1], got_2.at[step, 1], 2, step, across)

    def second(step):
        arrive(got_2.at[step, 0], 1, step)
        arrive(got_2.at[step, 1], 2, step)
        for index in range(2):
            part_2[step, 0, index] = add(part_1[step, index, col, 0], got_2[step, 0, index])
            part_2[step, 1, index] = add(part_1[step, row, index, 1], got_2[step, 1, index])
        send(part_2.at[step, 0, 1 - row], got_3.at[step, 0], 3, step, across)
        send(part_2.at[step, 1, 1 - col], got_3.at[step, 1], 4, step, beside)

    def third(step):
        arrive(got_3.at[step, 0], 3, step)
        arrive(got_3.at[step, 1], 4, step)
        part_3[step, 0] = add(part_2[step, 0, row], got_3[step, 0])
        part_3[step, 1] = add(part_2[step, 1, col], got_3[step, 1])
        if step:
            send(part_3.at[step], got_4.at[step], 5, step, spans[step - 1])

    for tick in range(n_ctx + 2):
        if tick < n_ctx:
            first(order[tick])
        if 0 <= tick - 1 < n_ctx:
            second(order[tick - 1])
        if 0 <= tick - 2 < n_ctx:
            third(order[tick - 2])
    for step in range(1, n_ctx):
        arrive(got_4.at[step], 5, step)
    for half in range(2):
        total = part_3[0, half].astype(jnp.float32)
        for step in range(1, n_ctx):
            total = total + got_4[step, half].astype(jnp.float32)
        sum_ref[half] = total
    if with_spans:
        for copy in span_copies:
            copy.wait_recv()
        total = span_ref[ctx].astype(jnp.float32)
        for step in range(1, n_ctx):
            total = total + span_got[step].astype(jnp.float32)
        span_sum[...] = total
    for copy in sent:
        copy.wait_send()


def vmem_call(kernel, operands, out_shape, scratch, collective_id):
    whole = pl.BlockSpec(memory_space=pltpu.VMEM)
    return pl.pallas_call(
        kernel,
        out_shape=out_shape,
        in_specs=[whole] * len(operands),
        out_specs=[whole] * len(out_shape),
        scratch_shapes=scratch,
        compiler_params=pltpu.CompilerParams(
            collective_id=collective_id, has_side_effects=True, vmem_limit_bytes=VMEM_LIMIT
        ),
    )(*operands)


def own_plan():
    return lax.axis_size("dp") == 8 and lax.axis_size("ctx") == 4


def all_shards(packed, collective_id, own_span=None):
    n_dp, n_ctx = lax.axis_size("dp"), lax.axis_size("ctx")
    with_spans = own_span is not None
    if not own_plan():
        shards = lax.all_gather(packed, ("dp", "ctx"), axis=0).reshape(n_dp, n_ctx, *packed.shape)
        return shards, lax.all_gather(own_span, "ctx", axis=0) if with_spans else None
    sems = pltpu.SemaphoreType.DMA((6, n_ctx))
    span_sems = pltpu.SemaphoreType.DMA((n_ctx,))
    operands, scratch = [packed], [sems, sems]
    out_shape = [jax.ShapeDtypeStruct((n_ctx, 2, 2, 2) + packed.shape, packed.dtype)]
    if with_spans:
        operands.append(own_span)
        scratch += [span_sems, span_sems]
        out_shape.append(jax.ShapeDtypeStruct((n_ctx,) + own_span.shape, own_span.dtype))
    results = vmem_call(
        functools.partial(gather_kernel, n_ctx, with_spans),
        operands,
        out_shape,
        scratch,
        collective_id,
    )
    shards = results[0].transpose(2, 3, 1, 0, 4, 5, 6).reshape(n_dp, n_ctx, *packed.shape)
    return shards, results[1] if with_spans else None


def sum_shards(terms, collective_id, span_terms=None):
    n_dp, n_ctx = terms.shape[:2]
    shard = terms.shape[2:]
    with_spans = span_terms is not None
    if not own_plan():
        part = lax.psum_scatter(terms, "dp", scatter_dimension=0)
        total = lax.psum_scatter(part, "ctx", scatter_dimension=0).astype(jnp.float32)
        if not with_spans:
            return total, None
        return total, lax.psum_scatter(span_terms, "ctx", scatter_dimension=0).astype(jnp.float32)
    sems = pltpu.SemaphoreType.DMA((6, n_ctx))
    span_sems = pltpu.SemaphoreType.DMA((n_ctx,))
    operands = [terms.reshape(2, 2, 2, n_ctx, *shard).transpose(3, 2, 0, 1, 4, 5, 6)]
    out_shape = [jax.ShapeDtypeStruct(shard, jnp.float32)]
    scratch = [
        pltpu.VMEM((n_ctx, 2, 2) + shard, terms.dtype),
        pltpu.VMEM((n_ctx, 2, 2) + shard, terms.dtype),
        pltpu.VMEM((n_ctx, 2, 2) + shard[1:], terms.dtype),
        pltpu.VMEM((n_ctx, 2, 2) + shard[1:], terms.dtype),
        pltpu.VMEM((n_ctx,) + shard, terms.dtype),
        pltpu.VMEM((n_ctx,) + shard, terms.dtype),
        pltpu.VMEM((n_ctx,) + shard, terms.dtype),
        sems,
        sems,
    ]
    if with_spans:
        operands.append(span_terms)
        out_shape.append(jax.ShapeDtypeStruct(span_terms.shape[1:], jnp.float32))
        scratch += [pltpu.VMEM(span_terms.shape, span_terms.dtype), span_sems, span_sems]
    results = vmem_call(
        functools.partial(scatter_kernel, n_ctx, with_spans),
        operands,
        out_shape,
        scratch,
        collective_id,
    )
    return results[0], results[1] if with_spans else None


GAIN_ROWS = 8


def side_columns():
    return 16 if own_plan() else 0


def halves(packed):
    middle = packed.shape[-1] // 2
    return jnp.stack([packed[..., :middle], packed[..., middle:]], axis=-3)


def columns(shards, start, stop):
    middle = shards.shape[-1]
    if stop <= middle:
        return shards[..., 0, :, start:stop]
    if start >= middle:
        return shards[..., 1, :, start - middle : stop - middle]
    return jnp.concatenate(
        [shards[..., 0, :, start:], shards[..., 1, :, : stop - middle]], axis=-1
    )


def cut(shards, widths):
    parts, start = [], 0
    for width in widths:
        parts.append(columns(shards, start, start + width))
        start += width
    return parts


def joined_mat(part):
    n_dp, n_ctx, rows, width = part.shape
    return part.transpose(0, 2, 1, 3).reshape(n_dp * rows, n_ctx * width)


def grad_parts(item, rows):
    n_dp, n_ctx = lax.axis_size("dp"), lax.axis_size("ctx")
    return item.astype(jnp.bfloat16).reshape(n_dp, rows, n_ctx, -1).transpose(0, 2, 1, 3)


def head_slice(ref_value, head):
    return ref_value[:, head * HEAD_DIM : (head + 1) * HEAD_DIM]


def attend_kernel(reach_ref, query_ref, both_ref, mixed_ref, log_ref):
    n_ctx, span = both_ref.shape[0], query_ref.shape[1]
    shape = (span, span)
    ahead = lax.broadcasted_iota(jnp.int32, shape, 1) - lax.broadcasted_iota(jnp.int32, shape, 0)
    seq = pl.program_id(0)
    for head in range(HEADS):
        group = head // (HEADS // KV_HEADS)
        query = head_slice(query_ref[0], head)
        scaled = []
        for part in range(n_ctx):
            key = head_slice(both_ref[part, 0], group)
            raw = transposed_product(query, key) * HEAD_DIM ** (-0.5)
            scaled.append(jnp.where(ahead <= reach_ref[seq, part], raw, NEG_FILL))
        peak = functools.reduce(jnp.maximum, scaled)
        peak = jnp.max(peak, axis=-1, keepdims=True)
        exponent = [jnp.exp(item - peak) for item in scaled]
        total = jnp.sum(functools.reduce(jnp.add, exponent), axis=-1, keepdims=True)
        inverse = 1.0 / total
        mixed = jnp.zeros((span, HEAD_DIM), jnp.float32)
        for part in range(n_ctx):
            value = head_slice(both_ref[part, 0], KV_HEADS + group)
            probs = (exponent[part] * inverse).astype(jnp.bfloat16)
            mixed = mixed + jnp.dot(probs, value, preferred_element_type=jnp.float32)
        mixed_ref[0, :, head * HEAD_DIM : (head + 1) * HEAD_DIM] = mixed.astype(jnp.bfloat16)
        log_ref[0, :, head : head + 1] = peak + jnp.log(total)


def attend_back_kernel(reach_ref, query_ref, both_ref, d_mixed_ref, log_ref, d_query_ref, d_both_ref):
    n_ctx, span = both_ref.shape[0], query_ref.shape[1]
    shape = (span, span)
    ahead = lax.broadcasted_iota(jnp.int32, shape, 0) - lax.broadcasted_iota(jnp.int32, shape, 1)
    seq = pl.program_id(0)
    group_size = HEADS // KV_HEADS
    for group in range(KV_HEADS):
        key_terms = [jnp.zeros((span, HEAD_DIM), jnp.float32)] * n_ctx
        value_terms = [jnp.zeros((span, HEAD_DIM), jnp.float32)] * n_ctx
        for head in range(group * group_size, (group + 1) * group_size):
            query = head_slice(query_ref[0], head)
            d_mixed = head_slice(d_mixed_ref[0], head)
            log_total = log_ref[0, head : head + 1, :]
            probs, d_probs = [], []
            for part in range(n_ctx):
                key = head_slice(both_ref[part, 0], group)
                value = head_slice(both_ref[part, 0], KV_HEADS + group)
                raw = transposed_product(key, query) * HEAD_DIM ** (-0.5)
                raw = jnp.where(ahead <= reach_ref[seq, part], raw, NEG_FILL)
                probs.append(jnp.exp(raw - log_total))
                d_probs.append(transposed_product(value, d_mixed))
            delta = functools.reduce(jnp.add, [p * d for p, d in zip(probs, d_probs)])
            delta = jnp.sum(delta, axis=0, keepdims=True)
            d_query = jnp.zeros((span, HEAD_DIM), jnp.float32)
            for part in range(n_ctx):
                key = head_slice(both_ref[part, 0], group)
                low_probs = probs[part].astype(jnp.bfloat16)
                d_scores = HEAD_DIM ** (-0.5) * (probs[part] * (d_probs[part] - delta))
                d_scores = d_scores.astype(jnp.bfloat16)
                value_terms[part] = value_terms[part] + jnp.dot(
                    low_probs, d_mixed, preferred_element_type=jnp.float32
                )
                key_terms[part] = key_terms[part] + jnp.dot(
                    d_scores, query, preferred_element_type=jnp.float32
                )
                d_query = d_query + rows_product(d_scores, key)
            d_query_ref[0, :, head * HEAD_DIM : (head + 1) * HEAD_DIM] = d_query
        for part in range(n_ctx):
            for place, terms in ((group, key_terms), (KV_HEADS + group, value_terms)):
                d_both_ref[part, 0, :, place * HEAD_DIM : (place + 1) * HEAD_DIM] = terms[
                    part
                ].astype(jnp.bfloat16)


def attention_call(kernel, reach, query, both, extra, outs):
    seqs, span, width = query.shape
    n_ctx = both.shape[0]

    def spec(array):
        if array.ndim == 4:
            return pl.BlockSpec((n_ctx, 1) + array.shape[2:], lambda seq: (0, seq, 0, 0))
        return pl.BlockSpec((1,) + array.shape[1:], lambda seq: (seq, 0, 0))

    return pl.pallas_call(
        kernel,
        grid=(seqs,),
        out_shape=outs,
        in_specs=[pl.BlockSpec(memory_space=pltpu.SMEM)]
        + [spec(item) for item in (query, both, *extra)],
        out_specs=[spec(item) for item in outs],
        compiler_params=pltpu.CompilerParams(vmem_limit_bytes=VMEM_LIMIT),
    )(reach, query, both, *extra)


def product(left_mat, right_mat):
    return jnp.dot(left_mat, right_mat, preferred_element_type=jnp.float32)


def per_device(
    tokens,
    span_order,
    cotangent,
    query_weight,
    key_weight,
    value_weight,
    output_weight,
    gate_weight,
    up_weight,
    down_weight,
    attention_gain,
    feedforward_gain,
):
    n_dp, n_ctx = lax.axis_size("dp"), lax.axis_size("ctx")
    rows = query_weight.shape[0]
    q_width, kv_width = query_weight.shape[1], key_weight.shape[1]
    ff_width, side = gate_weight.shape[1], side_columns()
    blocks = down_weight.shape[1] // rows
    first_widths = (q_width, kv_width, kv_width, side)
    second_widths = (output_weight.shape[1] - side, ff_width, ff_width, blocks * down_weight.shape[0])
    seqs, span_len, model_width = tokens.shape[0] * tokens.shape[1], *tokens.shape[2:]
    row_count = seqs * span_len

    def pad_gains(one, two, width):
        gains = jnp.stack([one, two], axis=-2)
        pads = [(0, 0)] * (gains.ndim - 2) + [(0, GAIN_ROWS - 2), (0, width - rows)]
        return jnp.pad(gains, pads)

    first = jnp.concatenate(
        [query_weight, key_weight, value_weight, output_weight[:, :side]], axis=1
    )
    first = jnp.concatenate(
        [first, pad_gains(attention_gain, feedforward_gain, first.shape[1])], axis=0
    )
    first_shards, _ = all_shards(halves(first), 1)
    query_part, key_part, value_part, output_side = cut(first_shards, first_widths)
    query_mat = joined_mat(query_part[:, :, :rows])
    key_mat = joined_mat(key_part[:, :, :rows])
    value_mat = joined_mat(value_part[:, :, :rows])
    gain_part = columns(first_shards[:, 0], 0, rows)[:, rows:]
    attn_gain = gain_part[:, 0].reshape(-1).astype(jnp.float32)
    ffn_gain = gain_part[:, 1].reshape(-1).astype(jnp.float32)

    sequence = tokens.astype(jnp.float32).reshape(row_count, model_width)
    inverse_one = lax.rsqrt(jnp.mean(sequence * sequence, axis=-1, keepdims=True) + EPSILON)
    norm_one = sequence * inverse_one
    normed = (norm_one * attn_gain).astype(jnp.bfloat16)
    query_pre = product(normed, query_mat)
    key_pre = product(normed, key_mat)
    value_low = product(normed, value_mat).astype(jnp.bfloat16)
    order = span_order.reshape(seqs, n_ctx)
    own_span = lax.dynamic_index_in_dim(order, lax.axis_index("ctx"), axis=1, keepdims=True)
    reach = (own_span - order) * span_len
    query_pos = own_span * span_len + jnp.arange(span_len, dtype=jnp.int32)[None, :]
    cos_table, sin_table = angle_tables(query_pos)
    kv_all_width = KV_HEADS * HEAD_DIM
    query_rot = rotate(query_pre.reshape(seqs, span_len, HEADS, HEAD_DIM), cos_table, sin_table)
    query_rot = query_rot.astype(jnp.bfloat16).reshape(seqs, span_len, HEADS * HEAD_DIM)
    key_rot = rotate(key_pre.reshape(seqs, span_len, KV_HEADS, HEAD_DIM), cos_table, sin_table)
    key_rot = key_rot.astype(jnp.bfloat16).reshape(row_count, kv_all_width)

    down_side = down_weight.T.reshape(blocks, rows, -1).swapaxes(0, 1).reshape(rows, -1)
    second = jnp.concatenate(
        [output_weight[:, side:], gate_weight, up_weight, down_side], axis=1
    )
    second = halves(jnp.pad(second, ((0, GAIN_ROWS), (0, 0))))
    second_shards, both_all = all_shards(
        second, 2, jnp.concatenate([key_rot, value_low], axis=-1)
    )
    output_rest, gate_part, up_part, down_part = cut(second_shards[..., :rows, :], second_widths)
    output_mat = joined_mat(jnp.concatenate([output_side[:, :, :rows], output_rest], axis=-1))
    gate_mat, up_mat = joined_mat(gate_part), joined_mat(up_part)
    down_mat = down_part.reshape(n_dp, n_ctx, rows, blocks, -1).transpose(1, 3, 2, 0, 4)
    down_mat = down_mat.reshape(model_width, -1)

    both_all = both_all.reshape(n_ctx, seqs, span_len, 2 * kv_all_width)
    mixed, log_total = attention_call(
        attend_kernel,
        reach,
        query_rot,
        both_all,
        (),
        [
            jax.ShapeDtypeStruct(query_rot.shape, jnp.bfloat16),
            jax.ShapeDtypeStruct((seqs, span_len, HEADS), jnp.float32),
        ],
    )
    mixed = mixed.reshape(row_count, HEADS * HEAD_DIM)
    middle = sequence + product(mixed, output_mat)
    inverse_two = lax.rsqrt(jnp.mean(middle * middle, axis=-1, keepdims=True) + EPSILON)
    norm_two = middle * inverse_two
    hidden = (norm_two * ffn_gain).astype(jnp.bfloat16)
    gate_act = product(hidden, gate_mat)
    up_act = product(hidden, up_mat)
    sigmoid_gate = jax.nn.sigmoid(gate_act)
    inner = (gate_act * sigmoid_gate * up_act).astype(jnp.bfloat16)
    layer_output = (middle + transposed_product(inner, down_mat)).astype(jnp.bfloat16)

    cot_rows = cotangent.reshape(row_count, model_width)
    d_inner = product(cot_rows, down_mat)
    silu_slope = sigmoid_gate + gate_act * sigmoid_gate * (1.0 - sigmoid_gate)
    d_gate = (d_inner * up_act * silu_slope).astype(jnp.bfloat16)
    d_up = (d_inner * (gate_act * sigmoid_gate)).astype(jnp.bfloat16)
    d_hidden = transposed_product(d_gate, gate_mat) + transposed_product(d_up, up_mat)
    ffn_gain_grad = jnp.sum(d_hidden * norm_two, axis=0)
    d_norm_two = d_hidden * ffn_gain
    d_middle = cot_rows.astype(jnp.float32) + inverse_two * (
        d_norm_two - norm_two * jnp.mean(d_norm_two * norm_two, axis=-1, keepdims=True)
    )
    d_branch = d_middle.astype(jnp.bfloat16)
    d_mixed = transposed_product(d_branch, output_mat).astype(jnp.bfloat16)
    d_query_rot, d_both = attention_call(
        attend_back_kernel,
        reach,
        query_rot,
        both_all,
        (d_mixed.reshape(query_rot.shape), jnp.swapaxes(log_total, 1, 2)),
        [
            jax.ShapeDtypeStruct(query_rot.shape, jnp.float32),
            jax.ShapeDtypeStruct(both_all.shape, jnp.bfloat16),
        ],
    )
    output_terms = grad_parts(rows_product(mixed, d_branch), rows)
    down_terms = rows_product(cot_rows, inner).astype(jnp.bfloat16)
    down_terms = down_terms.reshape(n_ctx, blocks, rows, n_dp, -1).transpose(3, 0, 2, 1, 4)
    second_terms = jnp.concatenate(
        [
            output_terms[..., side:],
            grad_parts(rows_product(hidden, d_gate), rows),
            grad_parts(rows_product(hidden, d_up), rows),
            down_terms.reshape(n_dp, n_ctx, rows, -1),
        ],
        axis=-1,
    )
    second_terms = jnp.pad(second_terms, ((0, 0), (0, 0), (0, GAIN_ROWS), (0, 0)))
    second_sum, both_sum = sum_shards(
        halves(second_terms), 3, d_both.reshape(n_ctx, row_count, 2 * kv_all_width)
    )
    output_grad, gate_grad, up_grad, down_grad = cut(second_sum[:, :rows], second_widths)
    down_grad = down_grad.reshape(rows, blocks, -1).swapaxes(0, 1).reshape(blocks * rows, -1).T

    d_query = unrotate(
        d_query_rot.reshape(seqs, span_len, HEADS, HEAD_DIM), cos_table, sin_table
    )
    d_query = d_query.reshape(row_count, HEADS * HEAD_DIM).astype(jnp.bfloat16)
    d_key = unrotate(
        both_sum[:, :kv_all_width].reshape(seqs, span_len, KV_HEADS, HEAD_DIM),
        cos_table,
        sin_table,
    )
    d_key = d_key.reshape(row_count, kv_all_width).astype(jnp.bfloat16)
    d_value = both_sum[:, kv_all_width:].astype(jnp.bfloat16)
    d_normed = (
        transposed_product(d_query, query_mat)
        + transposed_product(d_key, key_mat)
        + transposed_product(d_value, value_mat)
    )
    attn_gain_grad = jnp.sum(d_normed * norm_one, axis=0)
    d_norm_one = d_normed * attn_gain
    input_grad = d_middle + inverse_one * (
        d_norm_one - norm_one * jnp.mean(d_norm_one * norm_one, axis=-1, keepdims=True)
    )
    first_terms = jnp.concatenate(
        [
            grad_parts(rows_product(normed, d_query), rows),
            grad_parts(rows_product(normed, d_key), rows),
            grad_parts(rows_product(normed, d_value), rows),
            output_terms[..., :side],
        ],
        axis=-1,
    )
    gain_terms = pad_gains(
        attn_gain_grad.reshape(n_dp, rows).astype(jnp.bfloat16),
        ffn_gain_grad.reshape(n_dp, rows).astype(jnp.bfloat16),
        first_terms.shape[-1],
    )
    gain_terms = jnp.broadcast_to(gain_terms[:, None], (n_dp, n_ctx) + gain_terms.shape[1:])
    first_sum, _ = sum_shards(halves(jnp.concatenate([first_terms, gain_terms], axis=2)), 4)
    query_grad, key_grad, value_grad, side_grad = cut(first_sum[:, :rows], first_widths)
    output_grad = jnp.concatenate([side_grad, output_grad], axis=-1)
    gain_sums = columns(first_sum, 0, rows)[rows:]
    return (
        layer_output.reshape(tokens.shape),
        input_grad.reshape(tokens.shape),
        query_grad,
        key_grad,
        value_grad,
        output_grad,
        gate_grad,
        up_grad,
        down_grad,
        gain_sums[0],
        gain_sums[1],
    )


def solution(mesh):
    in_specs = (
        P(None, "dp", "ctx", None),
        P(None, "dp", None),
        P(None, "dp", "ctx", None),
        P("dp", "ctx"),
        P("dp", "ctx"),
        P("dp", "ctx"),
        P("dp", "ctx"),
        P("dp", "ctx"),
        P("dp", "ctx"),
        P("dp", "ctx"),
        P("dp"),
        P("dp"),
    )
    out_specs = (
        P(None, "dp", "ctx", None),
        P(None, "dp", "ctx", None),
        P("dp", "ctx"),
        P("dp", "ctx"),
        P("dp", "ctx"),
        P("dp", "ctx"),
        P("dp", "ctx"),
        P("dp", "ctx"),
        P("dp", "ctx"),
        P("dp"),
        P("dp"),
    )
    return jax.shard_map(
        per_device, mesh=mesh, in_specs=in_specs, out_specs=out_specs, check_vma=False
    )
```
